32 devices in a mesh: heads: 2 (over x), seq: 16 (over z, y, core).
Axes of the slice: x: 2, y: 2, z: 4, core: 2. Of those that a mesh axis runs over, the one named last changes fastest.
Arguments:
- queries: bfloat16 [8192, 4096], P('seq', 'heads'), may hold values from -6 to 6
- key_vectors: bfloat16 [8192, 4096], P('seq', 'heads'), may hold values from -6 to 6
- values: bfloat16 [8192, 4096], P('seq', 'heads'), may hold values from -40 to 40
- level_weights: float32 [14, 32, 8192], P(None, 'heads', 'seq'), may hold values from 0.1 to 1
- gate_branch: bfloat16 [8192, 4096], P(('seq', 'heads')), may hold values from -6 to 6
- norm_gain: float32 [4096], replicated, may hold values from 0.5 to 1.5
Outputs:
- normed: bfloat16 [8192, 4096], P(('seq', 'heads'))
The draws below stay inside these ranges and needn't reach their ends.
All inputs are finite; a program needn't handle non-finite values.
Results may differ from the reference program's by a relative error of at most 0.008.
Values may be sent and summed in bfloat16 or wider, within the bound.
No kernel may reach another device: no remote copies, remote signals or barrier semaphores. Data moves between devices by JAX's collectives and lax.ppermute only.
A program may use at most 128 MiB of HBM per device.

```python
import math
import jax
import jax.numpy as jnp
from jax import lax

HEADS = 32
HEAD_DIM = 128
WINDOW = 512
TOK_DEV = 512
MODEL = 4096
TOKENS = 8192
NEAR_LEVELS = 10
FAR_LEVELS = 4
LEVELS = 14


def draw_queries(key, part):
    noise_key = jax.random.fold_in(key, 1)
    field = jnp.clip(1.4 * jax.random.normal(noise_key, (TOKENS, MODEL), jnp.float32), -6.0, 6.0)
    return field.astype(jnp.bfloat16)


def draw_key_vectors(key, part):
    noise_key = jax.random.fold_in(key, 2)
    field = jnp.clip(1.4 * jax.random.normal(noise_key, (TOKENS, MODEL), jnp.float32), -6.0, 6.0)
    return field.astype(jnp.bfloat16)


def draw_values(key, part):
    noise_key = jax.random.fold_in(key, 3)
    field = jnp.clip(jax.random.normal(noise_key, (TOKENS, MODEL), jnp.float32), -6.0, 6.0)
    return field.astype(jnp.bfloat16)


def level_of(stream_key, dims, cuts, least, largest):
    def one(dim, blocks):
        steps = jax.random.uniform(jax.random.fold_in(jax.random.fold_in(stream_key, 6), dim), (blocks,), jnp.float32, least / len(cuts), largest / len(cuts))
        return jnp.repeat(jnp.exp(steps), dims[dim] // blocks).reshape((-1,) + (1,) * (len(dims) - dim - 1))

    factor_of = one(*cuts[0])
    for cut in cuts[1:]:
        factor_of = factor_of * one(*cut)
    return factor_of


def gaussian(stream_key, shape, spread, most, pieces=(), held_as=jnp.bfloat16):
    values = jax.random.normal(stream_key, shape, jnp.float32) * spread
    if len(pieces) > 0:
        values = level_of(stream_key, shape, pieces, -0.22, 0.18) * values
    return jnp.clip(values, min=-most, max=most).astype(held_as)


def setup_inputs(seed: int = 0) -> dict:
    splits = jax.random.split(jax.random.key(seed), 7)
    return {
        "queries": draw_queries(jax.random.fold_in(splits[6], 71), 0),
        "key_vectors": draw_key_vectors(jax.random.fold_in(splits[6], 71), 0),
        "values": draw_values(jax.random.fold_in(splits[6], 71), 0),
        "level_weights": jnp.clip(jnp.exp(math.log(1.0) - 2.3025851 * jax.random.uniform(splits[3], (LEVELS, HEADS, TOKENS), jnp.float32) ** level_of(splits[3], (LEVELS, HEADS, TOKENS), ((1, 2), (2, 16)), -0.2, 0.2)), 0.1, 1.0),
        "gate_branch": gaussian(splits[4], (TOKENS, MODEL), 1.0, 6.0, ((0, 32),)),
        "norm_gain": jnp.clip(1.0 + 0.1 * jax.random.normal(splits[5], (MODEL,), jnp.float32), 0.5, 1.5),
    }


EPSILON = 1e-06

def bit_count(numbers, width_bits):
    lengths = jnp.zeros(numbers.shape, jnp.int32)
    for shift_bit in range(width_bits):
        lengths = lengths + (numbers >> shift_bit > 0).astype(jnp.int32)
    return lengths

def level_scale(levels):
    return jnp.exp2(-0.5 * jnp.maximum(levels - 1, 0).astype(jnp.float32))

def reference(queries, key_vectors, values, level_weights, gate_branch, norm_gain):
    block_count = TOKENS // TOK_DEV
    score_scale = HEAD_DIM ** (-0.5)
    positions = jnp.arange(TOK_DEV, dtype=jnp.int32)
    level_table = bit_count(positions[:, None] ^ positions[None, :], NEAR_LEVELS)
    causal = positions[:, None] >= positions[None, :]
    near_scale = level_scale(jnp.arange(NEAR_LEVELS, dtype=jnp.int32))
    far_scale = level_scale(NEAR_LEVELS + jnp.arange(FAR_LEVELS, dtype=jnp.int32)) * score_scale
    block_ids = jnp.arange(block_count, dtype=jnp.int32)
    context_pos = jnp.arange(WINDOW + TOK_DEV, dtype=jnp.int32)

    def one_head(operands):
        query_head, key_head, value_head, weight_head = operands
        key_blocks = key_head.reshape(block_count, TOK_DEV, HEAD_DIM).astype(jnp.float32)
        value_blocks = value_head.reshape(block_count, TOK_DEV, HEAD_DIM).astype(jnp.float32)
        block_states = jnp.einsum('btd,bte->bde', key_blocks, value_blocks, precision=lax.Precision.HIGHEST).astype(jnp.bfloat16)
        state_float = lax.optimization_barrier(block_states).astype(jnp.float32)
        bucket_list = []
        for level_id in range(FAR_LEVELS):
            group_size = 2 ** level_id
            group_sums = state_float.reshape(block_count // group_size, group_size, HEAD_DIM, HEAD_DIM).sum(axis=1)
            sibling = jnp.maximum((block_ids >> level_id) - 1, 0)
            present = (block_ids >> level_id & 1).astype(jnp.float32)
            bucket_list.append(group_sums[sibling] * present[:, None, None])
        buckets = jnp.stack(bucket_list, axis=1).astype(jnp.bfloat16)
        padded_keys = jnp.concatenate([jnp.zeros((WINDOW, HEAD_DIM), jnp.bfloat16), key_head], axis=0)
        padded_values = jnp.concatenate([jnp.zeros((WINDOW, HEAD_DIM), jnp.bfloat16), value_head], axis=0)

        def one_block(block_id):
            first_token = block_id * TOK_DEV
            query_block = lax.dynamic_slice_in_dim(query_head, first_token, TOK_DEV, 0)
            context_keys = lax.dynamic_slice_in_dim(padded_keys, first_token, WINDOW + TOK_DEV, 0)
            context_values = lax.dynamic_slice_in_dim(padded_values, first_token, WINDOW + TOK_DEV, 0)
            block_weights = lax.dynamic_slice_in_dim(weight_head, first_token, TOK_DEV, 1)
            scores = jnp.dot(query_block, context_keys.T, preferred_element_type=jnp.float32) * score_scale
            key_pos = first_token - WINDOW + context_pos
            pos_gap = positions[:, None] + WINDOW - context_pos[None, :]
            in_window = (pos_gap >= 0) & (pos_gap < WINDOW) & (key_pos >= 0)[None, :]
            row_max = lax.optimization_barrier(jnp.max(jnp.where(in_window, scores, -jnp.inf), axis=1, keepdims=True))
            exp_scores = jnp.where(in_window, jnp.exp(scores - row_max), 0.0)
            weights = (exp_scores / lax.optimization_barrier(jnp.sum(exp_scores, axis=1, keepdims=True))).astype(jnp.bfloat16)
            windowed = jnp.dot(weights, context_values, preferred_element_type=jnp.float32)
            level_mix = jnp.zeros((TOK_DEV, TOK_DEV), jnp.float32)
            for level_id in range(NEAR_LEVELS):
                level_mix = level_mix + jnp.where(level_table == level_id, (block_weights[level_id] * near_scale[level_id])[:, None], 0.0)
            level_mix = jnp.where(causal, level_mix, 0.0)
            near_weights = (scores[:, WINDOW:] * level_mix).astype(jnp.bfloat16)
            near_out = jnp.dot(near_weights, context_values[WINDOW:], preferred_element_type=jnp.float32)
            block_buckets = buckets[block_id]
            far_proj = jnp.einsum('td,jde->jte', query_block.astype(jnp.float32), block_buckets.astype(jnp.float32), precision=lax.Precision.HIGHEST)
            far_coef = block_weights[NEAR_LEVELS:] * far_scale[:, None]
            far_out = lax.optimization_barrier(jnp.sum(far_coef[:, :, None] * far_proj, axis=0))
            return windowed + near_out + far_out
        return lax.map(one_block, block_ids).reshape(TOKENS, HEAD_DIM)
    query_heads = queries.reshape(TOKENS, HEADS, HEAD_DIM).transpose(1, 0, 2)
    key_heads = key_vectors.reshape(TOKENS, HEADS, HEAD_DIM).transpose(1, 0, 2)
    value_heads = values.reshape(TOKENS, HEADS, HEAD_DIM).transpose(1, 0, 2)
    head_outputs = lax.map(one_head, (query_heads, key_heads, value_heads, level_weights.transpose(1, 0, 2)))
    mixed = head_outputs.transpose(1, 0, 2).reshape(TOKENS, MODEL).astype(jnp.bfloat16)
    gated = mixed.astype(jnp.float32) * jax.nn.silu(gate_branch.astype(jnp.float32))
    mean_square = lax.optimization_barrier(jnp.mean(gated * gated, axis=1, keepdims=True))
    return (norm_gain * gated * lax.rsqrt(mean_square + EPSILON)).astype(jnp.bfloat16)
```

```python
import functools

import jax
import jax.numpy as jnp
from jax import lax
from jax.experimental import pallas as pl
from jax.experimental.pallas import tpu as pltpu
from jax.sharding import PartitionSpec as P

HEAD_DIM = 128
WINDOW = 512
EPSILON = 1e-06
LOG2E = 1.4426950408889634
VMEM = 48 * 1024 * 1024
NN = (((1,), (0,)), ((), ()))
NT = (((1,), (1,)), ((), ()))
TN = (((0,), (0,)), ((), ()))


def mm(left, right, dims=NN):
    return lax.dot_general(left, right, dims, preferred_element_type=jnp.float32)


def level_scale(levels):
    return jnp.exp2(-0.5 * jnp.maximum(levels - 1, 0).astype(jnp.float32))


def joined(parts, axis):
    return parts[0] if len(parts) == 1 else jnp.concatenate(parts, axis)


def state_kernel(heads, k_ref, v_ref, out_ref):
    for h in range(heads):
        cols = slice(h * HEAD_DIM, (h + 1) * HEAD_DIM)
        out_ref[h] = mm(k_ref[:, cols], v_ref[:, cols], TN).astype(jnp.bfloat16)


def block_states(k, v):
    rows, width = k.shape
    heads = width // HEAD_DIM
    step = 4 if heads % 4 == 0 else 1
    block = pl.BlockSpec((rows, step * HEAD_DIM), lambda g: (0, g))
    return pl.pallas_call(
        functools.partial(state_kernel, step),
        grid=(heads // step,),
        in_specs=[block, block],
        out_specs=pl.BlockSpec((step, HEAD_DIM, HEAD_DIM), lambda g: (g, 0, 0)),
        out_shape=jax.ShapeDtypeStruct((heads, HEAD_DIM, HEAD_DIM), jnp.bfloat16),
        name="block_states",
    )(k, v)


def attend_kernel(qb, first_ref, q_ref, k_ref, v_ref, kp_ref, vp_ref, lw_ref, table_ref, out_ref):
    rows = q_ref.shape[0]
    lane = HEAD_DIM
    scale = HEAD_DIM**-0.5 * LOG2E
    bias = jnp.where(first_ref[0] == 0, -1e30, 0.0).astype(jnp.float32)
    table = table_ref[...]
    causal = lax.broadcasted_iota(jnp.int32, (qb, qb), 0) >= lax.broadcasted_iota(
        jnp.int32, (qb, qb), 1
    )
    lane_bits = lane.bit_length() - 1
    lw = lw_ref[0]
    for low in range(0, rows, qb):
        high = low + qb
        q = q_ref[low:high, :]
        own = mm(q, k_ref[:high, :], NT)
        past = mm(q, kp_ref[low:, :], NT)
        edge = jnp.where(causal, own[:, low:], past[:, :qb] + bias)
        top = jnp.max(edge, axis=1, keepdims=True)
        if low:
            top = jnp.maximum(top, jnp.max(own[:, :low], axis=1, keepdims=True))
        if high < rows:
            top = jnp.maximum(top, jnp.max(past[:, qb:], axis=1, keepdims=True) + bias)
        edge = jnp.exp2((edge - top) * scale)
        total = jnp.sum(edge, axis=1, keepdims=True)
        own_weights = [jnp.where(causal, edge, 0.0).astype(jnp.bfloat16)]
        past_weights = [jnp.where(causal, 0.0, edge).astype(jnp.bfloat16)]
        if low:
            inner = jnp.exp2((own[:, :low] - top) * scale)
            total = total + jnp.sum(inner, axis=1, keepdims=True)
            own_weights.insert(0, inner.astype(jnp.bfloat16))
        if high < rows:
            outer = jnp.exp2((past[:, qb:] - (top - bias)) * scale)
            total = total + jnp.sum(outer, axis=1, keepdims=True)
            past_weights.append(outer.astype(jnp.bfloat16))
        windowed = mm(joined(own_weights, 1), v_ref[:high, :])
        windowed = windowed + mm(joined(past_weights, 1), vp_ref[low:, :])
        near_rows = []
        for a in range(low // lane, high // lane):
            inside = slice(a * lane - low, (a + 1) * lane - low)
            mix = lw[:, a * lane : (a + 1) * lane]
            mix = joined([mix, jnp.zeros((lane - mix.shape[0], lane), jnp.float32)], 0).T
            parts = []
            for b in range(high // lane):
                scores = own[inside, b * lane : (b + 1) * lane]
                if b < a:
                    level = lane_bits + (a ^ b).bit_length()
                    parts.append((scores * mix[:, level : level + 1]).astype(jnp.bfloat16))
                elif b == a:
                    picked = jnp.take_along_axis(mix, table, axis=1)
                    parts.append((scores * picked).astype(jnp.bfloat16))
                else:
                    parts.append(jnp.zeros((lane, lane), jnp.bfloat16))
            near_rows.append(joined(parts, 1))
        near = mm(joined(near_rows, 0), v_ref[:high, :])
        out_ref[low:high, :] = windowed * (1.0 / total) + near


def attend(first, q, k, v, past_k, past_v, lw, table, head):
    rows, width = past_k.shape
    whole = pl.BlockSpec((rows, HEAD_DIM), lambda g, *_: (0, head + g))
    part = pl.BlockSpec((rows, HEAD_DIM), lambda g, *_: (0, g))
    qb = min(rows, 256)
    return pl.pallas_call(
        functools.partial(attend_kernel, qb),
        grid_spec=pltpu.PrefetchScalarGridSpec(
            num_scalar_prefetch=1,
            grid=(width // HEAD_DIM,),
            in_specs=[
                whole,
                whole,
                whole,
                part,
                part,
                pl.BlockSpec((1,) + lw.shape[1:], lambda g, *_: (head + g, 0, 0)),
                pl.BlockSpec(table.shape, lambda g, *_: (0, 0)),
            ],
            out_specs=part,
        ),
        out_shape=jax.ShapeDtypeStruct((rows, width), jnp.float32),
        compiler_params=pltpu.CompilerParams(vmem_limit_bytes=VMEM),
        name="attend",
    )(first, q, k, v, past_k, past_v, lw, table)


def far_kernel(near_n, slots, place_ref, q_ref, lw_ref, bucket_ref, part_ref, *rest):
    out_refs, scratch = rest[:slots], rest[slots]
    rows = q_ref.shape[0]
    lane = HEAD_DIM
    far_n = bucket_ref.shape[0]
    lw = lw_ref[0]
    proj = mm(q_ref[...], joined([bucket_ref[j, 0] for j in range(far_n)], 1))
    for a in range(rows // lane):
        inside = slice(a * lane, (a + 1) * lane)
        mix = lw[:, inside]
        mix = joined([mix, jnp.zeros((lane - mix.shape[0], lane), jnp.float32)], 0).T
        total = part_ref[inside, :]
        for j in range(far_n):
            total = total + proj[inside, j * lane : (j + 1) * lane] * mix[:, near_n + j : near_n + j + 1]
        scratch[inside, :] = total
    count = rows // slots
    for s in range(slots):
        start = pl.multiple_of(lax.rem(place_ref[0] + s, slots) * count, count)
        out_refs[s][...] = scratch[pl.ds(start, count), :].astype(jnp.bfloat16)


def far(place, q, lw, buckets, part, head, near_n, slots):
    rows, width = part.shape
    far_n = buckets.shape[0]
    count = rows // slots
    return pl.pallas_call(
        functools.partial(far_kernel, near_n, slots),
        grid_spec=pltpu.PrefetchScalarGridSpec(
            num_scalar_prefetch=1,
            grid=(width // HEAD_DIM,),
            in_specs=[
                pl.BlockSpec((rows, HEAD_DIM), lambda g, *_: (0, head + g)),
                pl.BlockSpec((1,) + lw.shape[1:], lambda g, *_: (head + g, 0, 0)),
                pl.BlockSpec((far_n, 1, HEAD_DIM, HEAD_DIM), lambda g, *_: (0, head + g, 0, 0)),
                pl.BlockSpec((rows, HEAD_DIM), lambda g, *_: (0, g)),
            ],
            out_specs=[pl.BlockSpec((count, HEAD_DIM), lambda g, *_: (0, g))] * slots,
            scratch_shapes=[pltpu.VMEM((rows, HEAD_DIM), jnp.float32)],
        ),
        out_shape=[jax.ShapeDtypeStruct((count, width), jnp.bfloat16)] * slots,
        name="far",
    )(place, q, lw, buckets, part)


def norm_kernel(slots, offsets, local_width, place_ref, gate_ref, gain_ref, *rest):
    pieces, (out_ref, gated) = rest[:-2], rest[-2:]
    square = None
    index = 0
    for s in range(slots):
        base = lax.rem(place_ref[0] + slots - s, slots) * local_width
        for offset in offsets:
            piece = pieces[index]
            index += 1
            cols = pl.ds(pl.multiple_of(base + offset, HEAD_DIM), piece.shape[1])
            gate = gate_ref[:, cols].astype(jnp.float32)
            value = piece[...].astype(jnp.float32) * (gate / (1.0 + jnp.exp(-gate)))
            gated[:, cols] = value
            here = jnp.sum(value * value, axis=1, keepdims=True)
            square = here if square is None else square + here
    factor = lax.rsqrt(square / gated.shape[1] + EPSILON)
    out_ref[...] = (gain_ref[...] * gated[...] * factor).astype(jnp.bfloat16)


def norm(place, gate, gain, pieces, slots, offsets, local_width):
    rows, width = gate.shape
    tile = min(rows, 64)
    return pl.pallas_call(
        functools.partial(norm_kernel, slots, offsets, local_width),
        grid_spec=pltpu.PrefetchScalarGridSpec(
            num_scalar_prefetch=1,
            grid=(rows // tile,),
            in_specs=[
                pl.BlockSpec((tile, width), lambda g, *_: (g, 0)),
                pl.BlockSpec((1, width), lambda g, *_: (0, 0)),
            ]
            + [pl.BlockSpec((tile, p.shape[1]), lambda g, *_: (g, 0)) for p in pieces],
            out_specs=pl.BlockSpec((tile, width), lambda g, *_: (g, 0)),
            scratch_shapes=[pltpu.VMEM((tile, width), jnp.float32)],
        ),
        out_shape=jax.ShapeDtypeStruct((rows, width), jnp.bfloat16),
        compiler_params=pltpu.CompilerParams(vmem_limit_bytes=VMEM),
        name="norm",
    )(place, gate, gain.reshape(1, width), *pieces)


def shifted(value, axis, steps, wrap=False):
    count = lax.axis_size(axis)
    pairs = [(i, (i + steps) % count) for i in range(count) if wrap or i + steps < count]
    return lax.ppermute(value, axis, pairs)


def from_partner(value, axis, level, only_up=False):
    count = lax.axis_size(axis)
    pairs = [(i, i ^ 1 << level) for i in range(count) if not only_up or not i >> level & 1]
    return lax.ppermute(value, axis, pairs)


def added(left, right):
    return (left.astype(jnp.float32) + right.astype(jnp.float32)).astype(jnp.bfloat16)


def far_buckets(states, place, far_n):
    bit = [(place >> level & 1).astype(jnp.bfloat16) for level in range(far_n)]
    other = from_partner(states, "seq", 0)
    first = other * bit[0]
    if far_n == 1:
        return first[None]
    half = HEAD_DIM // 2
    running = added(states, other)
    running = lax.dynamic_slice_in_dim(running, (place & 1) * half, half, 1)
    halves = []
    for level in range(1, far_n):
        last = level == far_n - 1
        other = from_partner(running, "seq", level, last)
        halves.append(other * bit[level])
        if not last:
            running = added(running, other)
    mine = jnp.stack(halves, 0)
    theirs = from_partner(mine, "seq", 0)
    odd = place & 1 == 1
    rest = jnp.concatenate([jnp.where(odd, theirs, mine), jnp.where(odd, mine, theirs)], 2)
    return jnp.concatenate([first[None], rest], 0)


def local(queries, key_vectors, values, level_weights, gate_branch, norm_gain):
    rows, local_width = queries.shape
    heads = local_width // HEAD_DIM
    near_n = rows.bit_length()
    levels = level_weights.shape[0]
    far_n = levels - near_n
    slots = lax.axis_size("heads")
    seq_place = lax.axis_index("seq")
    first = seq_place.reshape(1)
    heads_place = lax.axis_index("heads").reshape(1)
    chunk = max(1, heads // 4)
    starts = list(range(0, heads, chunk))

    states = block_states(key_vectors, values)
    past = []
    for start in starts:
        cols = slice(start * HEAD_DIM, (start + chunk) * HEAD_DIM)
        past.append(shifted((key_vectors[:, cols], values[:, cols]), "seq", 1))
    buckets = far_buckets(states, seq_place, far_n)

    coef = level_scale(jnp.arange(levels, dtype=jnp.int32)) * HEAD_DIM**-0.5
    lw = jnp.transpose(level_weights, (1, 0, 2)) * coef[None, :, None]
    pos = jnp.arange(HEAD_DIM, dtype=jnp.int32)
    differ = pos[:, None] ^ pos[None, :]
    table = sum((differ >> b > 0).astype(jnp.int32) for b in range(HEAD_DIM.bit_length()))
    table = jnp.where(pos[:, None] >= pos[None, :], table, HEAD_DIM - 1)

    kept = [[] for _ in range(slots)]
    for start, (past_k, past_v) in zip(starts, past):
        part = attend(first, queries, key_vectors, values, past_k, past_v, lw, table, start)
        pieces = far(heads_place, queries, lw, buckets, part, start, near_n, slots)
        for s in range(slots):
            kept[s].append(pieces[s] if s == 0 else shifted(pieces[s], "heads", s, True))
    pieces = [piece for group in kept for piece in group]
    offsets = tuple(start * HEAD_DIM for start in starts)
    return norm(heads_place, gate_branch, norm_gain, pieces, slots, offsets, local_width)


def solution(mesh):
    return jax.shard_map(
        local,
        mesh=mesh,
        in_specs=(
            P("seq", "heads"),
            P("seq", "heads"),
            P("seq", "heads"),
            P(None, "heads", "seq"),
            P(("seq", "heads"), None),
            P(),
        ),
        out_specs=P(("seq", "heads"), None),
        check_vma=False,
    )
```

```python
import functools

import jax
import jax.numpy as jnp
from jax import lax
from jax.experimental import pallas as pl
from jax.experimental.pallas import tpu as pltpu
from jax.sharding import PartitionSpec as P

HEAD_DIM = 128
WINDOW = 512
EPSILON = 1e-06
LOG2E = 1.4426950408889634
VMEM = 24 * 1024 * 1024
NN = (((1,), (0,)), ((), ()))
NT = (((1,), (1,)), ((), ()))
TN = (((0,), (0,)), ((), ()))


def mm(left, right, dims=NN):
    return lax.dot_general(left, right, dims, preferred_element_type=jnp.float32)


def level_scale(levels):
    return jnp.exp2(-0.5 * jnp.maximum(levels - 1, 0).astype(jnp.float32))


def joined(parts, axis):
    return parts[0] if len(parts) == 1 else jnp.concatenate(parts, axis)


def state_kernel(heads, k_ref, v_ref, out_ref):
    for h in range(heads):
        cols = slice(h * HEAD_DIM, (h + 1) * HEAD_DIM)
        out_ref[h] = mm(k_ref[:, cols], v_ref[:, cols], TN).astype(jnp.bfloat16)


def block_states(k, v):
    rows, width = k.shape
    heads = width // HEAD_DIM
    step = 4 if heads % 4 == 0 else 1
    block = pl.BlockSpec((rows, step * HEAD_DIM), lambda g: (0, g))
    return pl.pallas_call(
        functools.partial(state_kernel, step),
        grid=(heads // step,),
        in_specs=[block, block],
        out_specs=pl.BlockSpec((step, HEAD_DIM, HEAD_DIM), lambda g: (g, 0, 0)),
        out_shape=jax.ShapeDtypeStruct((heads, HEAD_DIM, HEAD_DIM), jnp.bfloat16),
        name="block_states",
    )(k, v)


def attend_kernel(qb, heads, first_ref, q_ref, k_ref, v_ref, kp_ref, vp_ref, lw_ref, table_ref, out_ref):
    for h in range(heads):
        cols = slice(h * HEAD_DIM, (h + 1) * HEAD_DIM)
        tensors = [ref.at[:, cols] for ref in (q_ref, k_ref, v_ref, kp_ref, vp_ref)]
        attend_head(qb, first_ref, *tensors, lw_ref.at[h], table_ref, out_ref.at[:, cols])


def attend_head(qb, first_ref, q_ref, k_ref, v_ref, kp_ref, vp_ref, lw_ref, table_ref, out_ref):
    rows = q_ref.shape[0]
    lane = HEAD_DIM
    scale = HEAD_DIM**-0.5 * LOG2E
    bias = jnp.where(first_ref[0] == 0, -1e30, 0.0).astype(jnp.float32)
    table = table_ref[...]
    causal = lax.broadcasted_iota(jnp.int32, (qb, qb), 0) >= lax.broadcasted_iota(
        jnp.int32, (qb, qb), 1
    )
    lane_bits = lane.bit_length() - 1
    lw = lw_ref[...]
    for low in range(0, rows, qb):
        high = low + qb
        q = q_ref[low:high, :]
        own = mm(q, k_ref[:high, :], NT)
        past = mm(q, kp_ref[low:, :], NT)
        edge = jnp.where(causal, own[:, low:], past[:, :qb] + bias)
        top = jnp.max(edge, axis=1, keepdims=True)
        if low:
            top = jnp.maximum(top, jnp.max(own[:, :low], axis=1, keepdims=True))
        if high < rows:
            top = jnp.maximum(top, jnp.max(past[:, qb:], axis=1, keepdims=True) + bias)
        edge = jnp.exp2((edge - top) * scale)
        total = jnp.sum(edge, axis=1, keepdims=True)
        own_weights = [jnp.where(causal, edge, 0.0).astype(jnp.bfloat16)]
        past_weights = [jnp.where(causal, 0.0, edge).astype(jnp.bfloat16)]
        if low:
            inner = jnp.exp2((own[:, :low] - top) * scale)
            total = total + jnp.sum(inner, axis=1, keepdims=True)
            own_weights.insert(0, inner.astype(jnp.bfloat16))
        if high < rows:
            outer = jnp.exp2((past[:, qb:] - (top - bias)) * scale)
            total = total + jnp.sum(outer, axis=1, keepdims=True)
            past_weights.append(outer.astype(jnp.bfloat16))
        windowed = mm(joined(own_weights, 1), v_ref[:high, :])
        windowed = windowed + mm(joined(past_weights, 1), vp_ref[low:, :])
        near_rows = []
        for a in range(low // lane, high // lane):
            inside = slice(a * lane - low, (a + 1) * lane - low)
            mix = lw[:, a * lane : (a + 1) * lane]
            mix = joined([mix, jnp.zeros((lane - mix.shape[0], lane), jnp.float32)], 0).T
            parts = []
            for b in range(high // lane):
                scores = own[inside, b * lane : (b + 1) * lane]
                if b < a:
                    level = lane_bits + (a ^ b).bit_length()
                    parts.append((scores * mix[:, level : level + 1]).astype(jnp.bfloat16))
                elif b == a:
                    picked = jnp.take_along_axis(mix, table, axis=1)
                    parts.append((scores * picked).astype(jnp.bfloat16))
                else:
                    parts.append(jnp.zeros((lane, lane), jnp.bfloat16))
            near_rows.append(joined(parts, 1))
        near = mm(joined(near_rows, 0), v_ref[:high, :])
        out_ref[low:high, :] = windowed * (1.0 / total) + near


def heads_a_step(heads, most):
    return max(n for n in range(1, most + 1) if heads % n == 0)


def attend(first, q, k, v, past_k, past_v, lw, table, head, step):
    rows, width = past_k.shape
    cols = step * HEAD_DIM
    whole = pl.BlockSpec((rows, cols), lambda g, *_: (0, head // step + g))
    part = pl.BlockSpec((rows, cols), lambda g, *_: (0, g))
    qb = min(rows, 256)
    return pl.pallas_call(
        functools.partial(attend_kernel, qb, step),
        grid_spec=pltpu.PrefetchScalarGridSpec(
            num_scalar_prefetch=1,
            grid=(width // cols,),
            in_specs=[
                whole,
                whole,
                whole,
                part,
                part,
                pl.BlockSpec((step,) + lw.shape[1:], lambda g, *_: (head // step + g, 0, 0)),
                pl.BlockSpec(table.shape, lambda g, *_: (0, 0)),
            ],
            out_specs=part,
        ),
        out_shape=jax.ShapeDtypeStruct((rows, width), jnp.float32),
        compiler_params=pltpu.CompilerParams(vmem_limit_bytes=VMEM),
        name="attend",
    )(first, q, k, v, past_k, past_v, lw, table)


def far_kernel(near_n, slots, heads, far_n, place_ref, q_ref, lw_ref, part_ref, *rest):
    bucket_refs = rest[: 2 * far_n - 1]
    out_refs, scratch = rest[2 * far_n - 1 : -1], rest[-1]
    rows = q_ref.shape[0]
    lane = HEAD_DIM
    odd = place_ref[1] == 1
    for h in range(heads):
        cols = slice(h * lane, (h + 1) * lane)
        buckets = [bucket_refs[0][h]]
        for j in range(1, far_n):
            mine, theirs = bucket_refs[2 * j - 1][h], bucket_refs[2 * j][h]
            buckets += [jnp.where(odd, theirs, mine), jnp.where(odd, mine, theirs)]
        bucket = joined(buckets, 0)
        for a in range(rows // lane):
            inside = slice(a * lane, (a + 1) * lane)
            mix = lw_ref[h, :, inside]
            mix = joined([mix, jnp.zeros((lane - mix.shape[0], lane), jnp.float32)], 0).T
            q = q_ref[inside, cols].astype(jnp.float32)
            scaled = [
                (q * mix[:, near_n + j : near_n + j + 1]).astype(jnp.bfloat16) for j in range(far_n)
            ]
            scratch[inside, cols] = part_ref[inside, cols] + mm(joined(scaled, 1), bucket)
    count = rows // slots
    for s in range(slots):
        start = pl.multiple_of(lax.rem(place_ref[0] + s, slots) * count, count)
        out_refs[s][...] = scratch[pl.ds(start, count), :].astype(jnp.bfloat16)


def far(place, q, lw, buckets, part, head, near_n, slots, step):
    rows, width = part.shape
    far_n = (len(buckets) + 1) // 2
    count = rows // slots
    cols = step * HEAD_DIM
    group = lambda g, *_: (head // step + g, 0, 0)
    return pl.pallas_call(
        functools.partial(far_kernel, near_n, slots, step, far_n),
        grid_spec=pltpu.PrefetchScalarGridSpec(
            num_scalar_prefetch=1,
            grid=(width // cols,),
            in_specs=[
                pl.BlockSpec((rows, cols), lambda g, *_: (0, head // step + g)),
                pl.BlockSpec((step,) + lw.shape[1:], group),
                pl.BlockSpec((rows, cols), lambda g, *_: (0, g)),
            ]
            + [pl.BlockSpec((step,) + b.shape[1:], group) for b in buckets],
            out_specs=[pl.BlockSpec((count, cols), lambda g, *_: (0, g))] * slots,
            scratch_shapes=[pltpu.VMEM((rows, cols), jnp.float32)],
        ),
        out_shape=[jax.ShapeDtypeStruct((count, width), jnp.bfloat16)] * slots,
        compiler_params=pltpu.CompilerParams(vmem_limit_bytes=VMEM),
        name="far",
    )(place, q, lw, part, *buckets)


def norm_kernel(slots, offsets, local_width, place_ref, gate_ref, gain_ref, *rest):
    pieces, (out_ref, gated) = rest[:-2], rest[-2:]
    square = None
    index = 0
    for s in range(slots):
        base = lax.rem(place_ref[0] + slots - s, slots) * local_width
        for offset in offsets:
            piece = pieces[index]
            index += 1
            cols = pl.ds(pl.multiple_of(base + offset, HEAD_DIM), piece.shape[1])
            gate = gate_ref[:, cols].astype(jnp.float32)
            value = piece[...].astype(jnp.float32) * (gate / (1.0 + jnp.exp(-gate)))
            gated[:, cols] = value
            here = jnp.sum(value * value, axis=1, keepdims=True)
            square = here if square is None else square + here
    factor = lax.rsqrt(square / gated.shape[1] + EPSILON)
    out_ref[...] = (gain_ref[...] * gated[...] * factor).astype(jnp.bfloat16)


def norm(place, gate, gain, pieces, slots, offsets, local_width):
    rows, width = gate.shape
    tile = min(rows, 64)
    return pl.pallas_call(
        functools.partial(norm_kernel, slots, offsets, local_width),
        grid_spec=pltpu.PrefetchScalarGridSpec(
            num_scalar_prefetch=1,
            grid=(rows // tile,),
            in_specs=[
                pl.BlockSpec((tile, width), lambda g, *_: (g, 0)),
                pl.BlockSpec((1, width), lambda g, *_: (0, 0)),
            ]
            + [pl.BlockSpec((tile, p.shape[1]), lambda g, *_: (g, 0)) for p in pieces],
            out_specs=pl.BlockSpec((tile, width), lambda g, *_: (g, 0)),
            scratch_shapes=[pltpu.VMEM((tile, width), jnp.float32)],
        ),
        out_shape=jax.ShapeDtypeStruct((rows, width), jnp.bfloat16),
        compiler_params=pltpu.CompilerParams(vmem_limit_bytes=VMEM),
        name="norm",
    )(place, gate, gain.reshape(1, width), *pieces)


def shifted(value, axis, steps):
    count = lax.axis_size(axis)
    return lax.ppermute(value, axis, [(i, (i + steps) % count) for i in range(count)])


def from_partner(value, axis, level):
    return lax.ppermute(value, axis, [(i, i ^ 1 << level) for i in range(lax.axis_size(axis))])


def added(left, right):
    return (left.astype(jnp.float32) + right.astype(jnp.float32)).astype(jnp.bfloat16)


def after(value, *earlier):
    return lax.optimization_barrier((value,) + earlier)[0]


def local(queries, key_vectors, values, level_weights, gate_branch, norm_gain):
    rows, local_width = queries.shape
    heads = local_width // HEAD_DIM
    near_n = rows.bit_length()
    levels = level_weights.shape[0]
    far_n = levels - near_n
    slots = lax.axis_size("heads")
    seq_place = lax.axis_index("seq")
    first = seq_place.reshape(1)
    heads_place = lax.axis_index("heads")
    place = jnp.stack([heads_place, seq_place & 1])
    chunk = max(1, heads // 4)
    starts = list(range(0, heads, chunk))

    def halo(start, *earlier):
        cols = slice(start * HEAD_DIM, (start + chunk) * HEAD_DIM)
        pair = (key_vectors[:, cols], values[:, cols])
        if earlier:
            pair = lax.optimization_barrier(pair + earlier)[:2]
        return shifted(pair, "seq", 1)

    states = block_states(key_vectors, values)
    other = from_partner(states, "seq", 0)
    buckets = [other]
    half = HEAD_DIM // 2
    running = lax.dynamic_slice_in_dim(added(states, other), (seq_place & 1) * half, half, 1)
    past = []
    for level in range(1, far_n):
        other = from_partner(running, "seq", level)
        if level == far_n - 1:
            past += [halo(start, running) for start in starts[len(past) :]]
        elif len(past) < len(starts):
            past.append(halo(starts[len(past)], running))
        buckets += [other, from_partner(other, "seq", 0)]
        running = added(running, other)

    coef = level_scale(jnp.arange(levels, dtype=jnp.int32)) * HEAD_DIM**-0.5
    far_id = jnp.arange(levels, dtype=jnp.int32) - near_n
    present = jnp.where(far_id < 0, 1, seq_place >> jnp.maximum(far_id, 0) & 1)
    coef = coef * present.astype(jnp.float32)
    lw = jnp.transpose(level_weights, (1, 0, 2)) * coef[None, :, None]
    pos = jnp.arange(HEAD_DIM, dtype=jnp.int32)
    differ = pos[:, None] ^ pos[None, :]
    table = sum((differ >> b > 0).astype(jnp.int32) for b in range(HEAD_DIM.bit_length()))
    table = jnp.where(pos[:, None] >= pos[None, :], table, HEAD_DIM - 1)

    step = heads_a_step(chunk, 2)
    kept = [[] for _ in range(slots)]
    for start, (past_k, past_v) in zip(starts, past):
        part = attend(first, queries, key_vectors, values, past_k, past_v, lw, table, start, step)
        pieces = far(place, queries, lw, buckets, part, start, near_n, slots, step)
        for s in range(slots):
            kept[s].append(pieces[s] if s == 0 else shifted(pieces[s], "heads", s))
    pieces = [piece for group in kept for piece in group]
    offsets = tuple(start * HEAD_DIM for start in starts)
    return norm(heads_place.reshape(1), gate_branch, norm_gain, pieces, slots, offsets, local_width)


def solution(mesh):
    return jax.shard_map(
        local,
        mesh=mesh,
        in_specs=(
            P("seq", "heads"),
            P("seq", "heads"),
            P("seq", "heads"),
            P(None, "heads", "seq"),
            P(("seq", "heads"), None),
            P(),
        ),
        out_specs=P(("seq", "heads"), None),
        check_vma=False,
    )
```

```python
import functools

import jax
import jax.numpy as jnp
from jax import lax
from jax.experimental import pallas as pl
from jax.experimental.pallas import tpu as pltpu
from jax.sharding import PartitionSpec as P

HEAD_DIM = 128
WINDOW = 512
EPSILON = 1e-06
LOG2E = 1.4426950408889634
LEVEL_LANES = 16
SIZES = (1, 2, 1, 2, 1, 1)
VMEM = 24 * 1024 * 1024
NN = (((1,), (0,)), ((), ()))
NT = (((1,), (1,)), ((), ()))
TN = (((0,), (0,)), ((), ()))


def mm(left, right, dims=NN):
    return lax.dot_general(left, right, dims, preferred_element_type=jnp.float32)


def level_scale(levels):
    return jnp.exp2(-0.5 * jnp.maximum(levels - 1, 0).astype(jnp.float32))


def joined(parts, axis):
    return parts[0] if len(parts) == 1 else jnp.concatenate(parts, axis)


def cost(micros):
    return pl.CostEstimate(
        flops=int(micros * 1.1e9), bytes_accessed=int(micros * 3.6e6), transcendentals=0
    )


def state_kernel(heads, k_ref, v_ref, out_ref, copy_ref):
    for h in range(heads):
        cols = slice(h * HEAD_DIM, (h + 1) * HEAD_DIM)
        out_ref[h] = mm(k_ref[:, cols], v_ref[:, cols], TN).astype(jnp.bfloat16)

    @pl.when(pl.program_id(0) == 0)
    def _():
        copy_ref[0] = k_ref[:, : copy_ref.shape[2]]
        copy_ref[1] = v_ref[:, : copy_ref.shape[2]]


def block_states(k, v, copied):
    rows, width = k.shape
    heads = width // HEAD_DIM
    step = 4 if heads % 4 == 0 else 1
    block = pl.BlockSpec((rows, step * HEAD_DIM), lambda g: (0, g))
    copy_shape = (2, rows, copied * HEAD_DIM)
    return pl.pallas_call(
        functools.partial(state_kernel, step),
        grid=(heads // step,),
        in_specs=[block, block],
        out_specs=[pl.BlockSpec((step, HEAD_DIM, HEAD_DIM), lambda g: (g, 0, 0)), pl.BlockSpec(copy_shape, lambda g: (0, 0, 0))],
        out_shape=[
            jax.ShapeDtypeStruct((heads, HEAD_DIM, HEAD_DIM), jnp.bfloat16),
            jax.ShapeDtypeStruct(copy_shape, k.dtype),
        ],
        cost_estimate=cost(0.3 * heads),
        name="block_states",
    )(k, v)


def attend_kernel(qb, heads, near_n, slots, place_ref, q_ref, k_ref, v_ref, past_ref, lw_ref, table_ref, *rest):
    bucket_refs, out_refs, mixed = rest[: -1 - slots], rest[-1 - slots : -1], rest[-1]
    rows = q_ref.shape[0]
    odd = place_ref[1] == 1
    for h in range(heads):
        cols = slice(h * HEAD_DIM, (h + 1) * HEAD_DIM)
        buckets = [bucket_refs[0][h]]
        for mine_ref, theirs_ref in zip(bucket_refs[1::2], bucket_refs[2::2]):
            mine, theirs = mine_ref[h], theirs_ref[h]
            buckets += [jnp.where(odd, theirs, mine), jnp.where(odd, mine, theirs)]
        tensors = [ref.at[:, cols] for ref in (q_ref, k_ref, v_ref, past_ref.at[0], past_ref.at[1])]
        attend_head(qb, place_ref, *tensors, lw_ref, table_ref, joined(buckets, 0), mixed.at[:, cols], h, near_n)
    count = rows // slots
    for s in range(slots):
        start = pl.multiple_of(lax.rem(place_ref[0] + s, slots) * count, count)
        out_refs[s][...] = mixed[pl.ds(start, count), :].astype(jnp.bfloat16)


def attend_head(qb, place_ref, q_ref, k_ref, v_ref, kp_ref, vp_ref, lw_ref, table_ref, bucket, out_ref, head, near_n):
    rows = q_ref.shape[0]
    lane = HEAD_DIM
    scale = HEAD_DIM**-0.5 * LOG2E
    bias = jnp.where(place_ref[2] == 0, -1e30, 0.0).astype(jnp.float32)
    table = table_ref[head]
    causal = lax.broadcasted_iota(jnp.int32, (qb, qb), 0) >= lax.broadcasted_iota(
        jnp.int32, (qb, qb), 1
    )
    lane_bits = lane.bit_length() - 1
    first_level = head * LEVEL_LANES
    for low in range(0, rows, qb):
        high = low + qb
        q = q_ref[low:high, :]
        own = mm(q, k_ref[:high, :], NT)
        past = mm(q, kp_ref[low:, :], NT)
        edge = jnp.where(causal, own[:, low:], past[:, :qb] + bias)
        top = jnp.max(edge, axis=1, keepdims=True)
        if low:
            top = jnp.maximum(top, jnp.max(own[:, :low], axis=1, keepdims=True))
        if high < rows:
            top = jnp.maximum(top, jnp.max(past[:, qb:], axis=1, keepdims=True) + bias)
        edge = jnp.exp2((edge - top) * scale)
        total = jnp.sum(edge, axis=1, keepdims=True)
        own_weights = [jnp.where(causal, edge, 0.0).astype(jnp.bfloat16)]
        past_weights = [jnp.where(causal, 0.0, edge).astype(jnp.bfloat16)]
        if low:
            inner = jnp.exp2((own[:, :low] - top) * scale)
            total = total + jnp.sum(inner, axis=1, keepdims=True)
            own_weights.insert(0, inner.astype(jnp.bfloat16))
        if high < rows:
            outer = jnp.exp2((past[:, qb:] - (top - bias)) * scale)
            total = total + jnp.sum(outer, axis=1, keepdims=True)
            past_weights.append(outer.astype(jnp.bfloat16))
        windowed = mm(joined(own_weights, 1), v_ref[:high, :])
        windowed = windowed + mm(joined(past_weights, 1), vp_ref[low:, :])
        near_rows, far_rows = [], []
        far_n = bucket.shape[0] // lane
        for a in range(low // lane, high // lane):
            inside = slice(a * lane - low, (a + 1) * lane - low)
            mix = lw_ref[0, a * lane : (a + 1) * lane, :]
            parts = []
            for b in range(high // lane):
                scores = own[inside, b * lane : (b + 1) * lane]
                if b < a:
                    level = first_level + lane_bits + (a ^ b).bit_length()
                    parts.append((scores * mix[:, level : level + 1]).astype(jnp.bfloat16))
                elif b == a:
                    picked = jnp.take_along_axis(mix, table, axis=1)
                    parts.append((scores * picked).astype(jnp.bfloat16))
                else:
                    parts.append(jnp.zeros((lane, lane), jnp.bfloat16))
            near_rows.append(joined(parts, 1))
            q_part = q[inside, :].astype(jnp.float32)
            level = first_level + near_n
            far_parts = [
                (q_part * mix[:, level + j : level + j + 1]).astype(jnp.bfloat16) for j in range(far_n)
            ]
            far_rows.append(joined(far_parts, 1))
        near = mm(joined(near_rows, 0), v_ref[:high, :])
        near = near + mm(joined(far_rows, 0), bucket)
        out_ref[low:high, :] = windowed * (1.0 / total) + near


def attend(place, q, k, v, past, lw, table, buckets, head, step, near_n, slots):
    rows, width = past.shape[1:]
    cols = step * HEAD_DIM
    count = rows // slots
    whole = pl.BlockSpec((rows, cols), lambda g, *_: (0, head // step + g))
    group = lambda g, *_: (head // step + g, 0, 0)
    qb = min(rows, 256)
    return pl.pallas_call(
        functools.partial(attend_kernel, qb, step, near_n, slots),
        grid_spec=pltpu.PrefetchScalarGridSpec(
            num_scalar_prefetch=1,
            grid=(width // cols,),
            in_specs=[
                whole,
                whole,
                whole,
                pl.BlockSpec((2, rows, cols), lambda g, *_: (0, 0, g)),
                pl.BlockSpec((1,) + lw.shape[1:], group),
                pl.BlockSpec(table.shape, lambda g, *_: (0, 0, 0)),
            ]
            + [pl.BlockSpec((step,) + b.shape[1:], group) for b in buckets],
            out_specs=[pl.BlockSpec((count, cols), lambda g, *_: (0, g))] * slots,
            scratch_shapes=[pltpu.VMEM((rows, cols), jnp.float32)],
        ),
        out_shape=[jax.ShapeDtypeStruct((count, width), jnp.bfloat16)] * slots,
        compiler_params=pltpu.CompilerParams(vmem_limit_bytes=VMEM),
        cost_estimate=cost(1.6 * width / HEAD_DIM),
        name="attend",
    )(place, q, k, v, past, lw, table, *buckets)


def norm_kernel(slots, offsets, local_width, place_ref, gate_ref, gain_ref, *rest):
    pieces, (out_ref, gated) = rest[:-2], rest[-2:]
    square = None
    index = 0
    for s in range(slots):
        base = lax.rem(place_ref[0] + slots - s, slots) * local_width
        for offset in offsets:
            piece = pieces[index]
            index += 1
            cols = pl.ds(pl.multiple_of(base + offset, HEAD_DIM), piece.shape[1])
            gate = gate_ref[:, cols].astype(jnp.float32)
            value = piece[...].astype(jnp.float32) * (gate / (1.0 + jnp.exp(-gate)))
            gated[:, cols] = value
            here = jnp.sum(value * value, axis=1, keepdims=True)
            square = here if square is None else square + here
    factor = lax.rsqrt(square / gated.shape[1] + EPSILON)
    out_ref[...] = (gain_ref[...] * gated[...] * factor).astype(jnp.bfloat16)


def norm(place, gate, gain, pieces, slots, offsets, local_width):
    rows, width = gate.shape
    tile = min(rows, 64)
    return pl.pallas_call(
        functools.partial(norm_kernel, slots, offsets, local_width),
        grid_spec=pltpu.PrefetchScalarGridSpec(
            num_scalar_prefetch=1,
            grid=(rows // tile,),
            in_specs=[
                pl.BlockSpec((tile, width), lambda g, *_: (g, 0)),
                pl.BlockSpec((1, width), lambda g, *_: (0, 0)),
            ]
            + [pl.BlockSpec((tile, p.shape[1]), lambda g, *_: (g, 0)) for p in pieces],
            out_specs=pl.BlockSpec((tile, width), lambda g, *_: (g, 0)),
            scratch_shapes=[pltpu.VMEM((tile, width), jnp.float32)],
        ),
        out_shape=jax.ShapeDtypeStruct((rows, width), jnp.bfloat16),
        compiler_params=pltpu.CompilerParams(vmem_limit_bytes=VMEM),
        cost_estimate=cost(3.2),
        name="norm",
    )(place, gate, gain.reshape(1, width), *pieces)


def shifted(value, axis, steps):
    count = lax.axis_size(axis)
    return lax.ppermute(value, axis, [(i, (i + steps) % count) for i in range(count)])


def from_partner(value, axis, level):
    return lax.ppermute(value, axis, [(i, i ^ 1 << level) for i in range(lax.axis_size(axis))])


def added(left, right):
    return (left.astype(jnp.float32) + right.astype(jnp.float32)).astype(jnp.bfloat16)


def after(value, *earlier):
    return lax.optimization_barrier((value,) + earlier)[0]


def local(queries, key_vectors, values, level_weights, gate_branch, norm_gain):
    rows, local_width = queries.shape
    heads = local_width // HEAD_DIM
    near_n = rows.bit_length()
    levels = level_weights.shape[0]
    far_n = levels - near_n
    slots = lax.axis_size("heads")
    seq_place = lax.axis_index("seq")
    heads_place = lax.axis_index("heads")
    place = jnp.stack([heads_place, seq_place & 1, seq_place])
    unit = heads // 8
    sizes = [n * unit for n in SIZES] if heads % 8 == 0 else [1] * heads
    starts = [sum(sizes[:i]) for i in range(len(sizes))]
    step = min(sizes)

    coef = level_scale(jnp.arange(levels, dtype=jnp.int32)) * HEAD_DIM**-0.5
    far_id = jnp.arange(levels, dtype=jnp.int32) - near_n
    present = jnp.where(far_id < 0, 1, seq_place >> jnp.maximum(far_id, 0) & 1)
    coef = coef * present.astype(jnp.float32)
    lw = (level_weights * coef[:, None, None]).reshape(levels, heads // step, step, rows)
    lw = jnp.pad(jnp.transpose(lw, (1, 3, 2, 0)), ((0, 0), (0, 0), (0, 0), (0, LEVEL_LANES - levels)))
    lw = lw.reshape(heads // step, rows, step * LEVEL_LANES)
    lw = jnp.pad(lw, ((0, 0), (0, 0), (0, HEAD_DIM - step * LEVEL_LANES)))
    pos = jnp.arange(HEAD_DIM, dtype=jnp.int32)
    differ = pos[:, None] ^ pos[None, :]
    table = sum((differ >> b > 0).astype(jnp.int32) for b in range(HEAD_DIM.bit_length()))
    table = table + LEVEL_LANES * jnp.arange(step, dtype=jnp.int32)[:, None, None]
    table = jnp.where(pos[:, None] >= pos[None, :], table, HEAD_DIM - 1)

    past = []

    def send_until(count, *earlier):
        for index in range(len(past), min(count, len(sizes))):
            past.append(shifted(after(cuts[index], *earlier), "seq", 1))

    half = HEAD_DIM // 2
    states, cut = block_states(key_vectors, values, sizes[0])
    cuts = [cut]
    send_until(1)
    other = from_partner(states, "seq", 0)
    buckets = [other]
    running = lax.dynamic_slice_in_dim(added(states, other), (seq_place & 1) * half, half, 1)
    whole = lax.optimization_barrier((key_vectors, values, running))[:2]
    for start, size in zip(starts[1:], sizes[1:]):
        cols = slice(start * HEAD_DIM, (start + size) * HEAD_DIM)
        cuts.append(jnp.stack([w[:, cols] for w in whole]))
    for level in range(1, far_n):
        other = from_partner(running, "seq", level)
        if level < far_n - 1:
            send_until(1 + level, running)
            running = added(running, other)
        buckets += [other, from_partner(other, "seq", 0)]
    send_until(len(sizes), other)

    kept = [[] for _ in range(slots)]
    latest = ()
    for index in range(len(sizes)):
        pieces = attend(
            place, queries, key_vectors, values, after(past[index], *latest), lw, table, buckets,
            starts[index], step, near_n, slots,
        )
        latest = (pieces[-1],)
        for s in range(slots):
            kept[s].append(pieces[s] if s == 0 else shifted(pieces[s], "heads", s))
    pieces = [piece for group in kept for piece in group]
    offsets = tuple(start * HEAD_DIM for start in starts)
    return norm(heads_place.reshape(1), gate_branch, norm_gain, pieces, slots, offsets, local_width)


def solution(mesh):
    return jax.shard_map(
        local,
        mesh=mesh,
        in_specs=(
            P("seq", "heads"),
            P("seq", "heads"),
            P("seq", "heads"),
            P(None, "heads", "seq"),
            P(("seq", "heads"), None),
            P(),
        ),
        out_specs=P(("seq", "heads"), None),
        check_vma=False,
    )
```

```python
import functools

import jax
import jax.numpy as jnp
from jax import lax
from jax.experimental import pallas as pl
from jax.experimental.pallas import tpu as pltpu
from jax.sharding import PartitionSpec as P

HEAD_DIM = 128
WINDOW = 512
EPSILON = 1e-06
LOG2E = 1.4426950408889634
LEVEL_LANES = 16
SIZES = (1, 2, 2, 1, 1, 1)
VMEM = 16 * 1024 * 1024
NN = (((1,), (0,)), ((), ()))
NT = (((1,), (1,)), ((), ()))
TN = (((0,), (0,)), ((), ()))


def mm(left, right, dims=NN):
    return lax.dot_general(left, right, dims, preferred_element_type=jnp.float32)


def level_scale(levels):
    return jnp.exp2(-0.5 * jnp.maximum(levels - 1, 0).astype(jnp.float32))


def joined(parts, axis):
    return parts[0] if len(parts) == 1 else jnp.concatenate(parts, axis)


def cost(micros):
    return pl.CostEstimate(
        flops=int(micros * 1.1e9), bytes_accessed=int(micros * 3.6e6), transcendentals=0
    )


def state_kernel(heads, k_ref, v_ref, out_ref, copy_ref):
    for h in range(heads):
        cols = slice(h * HEAD_DIM, (h + 1) * HEAD_DIM)
        out_ref[h] = mm(k_ref[:, cols], v_ref[:, cols], TN).astype(jnp.bfloat16)

    @pl.when(pl.program_id(0) == 0)
    def _():
        copy_ref[0] = k_ref[:, : copy_ref.shape[2]]
        copy_ref[1] = v_ref[:, : copy_ref.shape[2]]


def block_states(k, v, copied):
    rows, width = k.shape
    heads = width // HEAD_DIM
    step = heads // 2 if heads % 2 == 0 else heads
    block = pl.BlockSpec((rows, step * HEAD_DIM), lambda g: (0, g))
    copy_shape = (2, rows, copied * HEAD_DIM)
    return pl.pallas_call(
        functools.partial(state_kernel, step),
        grid=(heads // step,),
        in_specs=[block, block],
        out_specs=[pl.BlockSpec((step, HEAD_DIM, HEAD_DIM), lambda g: (g, 0, 0)), pl.BlockSpec(copy_shape, lambda g: (0, 0, 0))],
        out_shape=[
            jax.ShapeDtypeStruct((heads, HEAD_DIM, HEAD_DIM), jnp.bfloat16),
            jax.ShapeDtypeStruct(copy_shape, k.dtype),
        ],
        cost_estimate=cost(0.3 * heads),
        name="block_states",
    )(k, v)


def attend_kernel(qb, heads, near_n, slots, place_ref, q_ref, k_ref, v_ref, past_ref, lw_ref, table_ref, *rest):
    bucket_refs, out_refs, mixed = rest[: -1 - slots], rest[-1 - slots : -1], rest[-1]
    rows = q_ref.shape[0]
    odd = place_ref[1] == 1
    for h in range(heads):
        cols = slice(h * HEAD_DIM, (h + 1) * HEAD_DIM)
        buckets = [bucket_refs[0][h]]
        for mine_ref, theirs_ref in zip(bucket_refs[1::2], bucket_refs[2::2]):
            mine, theirs = mine_ref[h], theirs_ref[h]
            buckets += [jnp.where(odd, theirs, mine), jnp.where(odd, mine, theirs)]
        tensors = [ref.at[:, cols] for ref in (q_ref, k_ref, v_ref, past_ref.at[0], past_ref.at[1])]
        attend_head(qb, place_ref, *tensors, lw_ref, table_ref, joined(buckets, 0), mixed.at[:, cols], h, near_n)
    count = rows // slots
    for s in range(slots):
        start = pl.multiple_of(lax.rem(place_ref[0] + s, slots) * count, count)
        out_refs[s][...] = mixed[pl.ds(start, count), :].astype(jnp.bfloat16)


def attend_head(qb, place_ref, q_ref, k_ref, v_ref, kp_ref, vp_ref, lw_ref, table_ref, bucket, out_ref, head, near_n):
    lane = HEAD_DIM
    scale = HEAD_DIM**-0.5 * LOG2E
    bias = jnp.where(place_ref[2] == 0, -1e30, 0.0).astype(jnp.float32)
    table = table_ref[head]
    causal = lax.broadcasted_iota(jnp.int32, (qb, qb), 0) >= lax.broadcasted_iota(
        jnp.int32, (qb, qb), 1
    )
    lane_bits = lane.bit_length() - 1
    first_level = head * LEVEL_LANES
    far_n = bucket.shape[0] // lane
    bf = jnp.bfloat16
    q = q_ref[...]
    own_low = mm(q, k_ref[:qb, :], NT)
    own_high = mm(q[qb:], k_ref[qb:, :], NT)
    past_low = mm(q[:qb], kp_ref[:qb, :], NT) + bias
    past_high = mm(q, kp_ref[qb:, :], NT) + bias

    def softmax(edge_own, edge_past, full):
        edge = jnp.where(causal, edge_own, edge_past)
        top = jnp.max(jnp.maximum(edge, full), axis=1, keepdims=True)
        edge = jnp.exp2((edge - top) * scale)
        full = jnp.exp2((full - top) * scale)
        total = jnp.sum(edge + full, axis=1, keepdims=True)
        own = jnp.where(causal, edge, 0.0).astype(bf)
        return own, jnp.where(causal, 0.0, edge).astype(bf), full.astype(bf), 1.0 / total

    low_own, low_past, low_full, low_factor = softmax(own_low[:qb], past_low, past_high[:qb])
    high_own, high_past, high_full, high_factor = softmax(own_high, past_high[qb:], own_low[qb:])

    def near_weights(scores, row, column):
        out = []
        for a in range(row // lane, row // lane + qb // lane):
            mix = lw_ref[0, a * lane : (a + 1) * lane, :]
            parts = []
            for b in range(column // lane, column // lane + qb // lane):
                part = scores[a * lane - row : (a + 1) * lane - row, b * lane - column : (b + 1) * lane - column]
                if b < a:
                    level = first_level + lane_bits + (a ^ b).bit_length()
                    parts.append((part * mix[:, level : level + 1]).astype(bf))
                elif b == a:
                    parts.append((part * jnp.take_along_axis(mix, table, axis=1)).astype(bf))
                else:
                    parts.append(jnp.zeros((lane, lane), bf))
            out.append(joined(parts, 1))
        return joined(out, 0)

    first = mm(
        joined(
            [low_own, high_full, near_weights(own_low[:qb], 0, 0), near_weights(own_low[qb:], qb, 0)], 0
        ),
        v_ref[:qb, :],
    )
    second = mm(joined([high_own, near_weights(own_high, qb, qb)], 0), v_ref[qb:, :])
    third = mm(low_past, vp_ref[:qb, :])
    fourth = mm(joined([low_full, high_past], 0), vp_ref[qb:, :])
    proj = mm(q, joined([bucket[j*lane:(j+1)*lane] for j in range(far_n)], 1))
    far_rows = []
    for a in range(2 * qb // lane):
        inside = slice(a * lane, (a + 1) * lane)
        mix = lw_ref[0, inside, :]
        level = first_level + near_n
        total = None
        for j in range(far_n):
            t = proj[inside, j*lane:(j+1)*lane] * mix[:, level + j : level + j + 1]
            total = t if total is None else total + t
        far_rows.append(total)
    far = joined(far_rows, 0)
    out_ref[:qb, :] = (first[:qb] + third + fourth[:qb]) * low_factor + first[2 * qb : 3 * qb] + far[:qb]
    out_ref[qb:, :] = (
        (first[qb : 2 * qb] + second[:qb] + fourth[qb:]) * high_factor
        + first[3 * qb :]
        + second[qb:]
        + far[qb:]
    )


def attend(place, q, k, v, past, lw, table, buckets, head, step, near_n, slots):
    rows, width = past.shape[1:]
    cols = step * HEAD_DIM
    count = rows // slots
    whole = pl.BlockSpec((rows, cols), lambda g, *_: (0, head // step + g))
    group = lambda g, *_: (head // step + g, 0, 0)
    qb = rows // 2
    return pl.pallas_call(
        functools.partial(attend_kernel, qb, step, near_n, slots),
        grid_spec=pltpu.PrefetchScalarGridSpec(
            num_scalar_prefetch=1,
            grid=(width // cols,),
            in_specs=[
                whole,
                whole,
                whole,
                pl.BlockSpec((2, rows, cols), lambda g, *_: (0, 0, g)),
                pl.BlockSpec((1,) + lw.shape[1:], group),
                pl.BlockSpec(table.shape, lambda g, *_: (0, 0, 0)),
            ]
            + [pl.BlockSpec((step,) + b.shape[1:], group) for b in buckets],
            out_specs=[pl.BlockSpec((count, cols), lambda g, *_: (0, g))] * slots,
            scratch_shapes=[pltpu.VMEM((rows, cols), jnp.float32)],
        ),
        out_shape=[jax.ShapeDtypeStruct((count, width), jnp.bfloat16)] * slots,
        compiler_params=pltpu.CompilerParams(vmem_limit_bytes=VMEM),
        cost_estimate=cost(1.6 * width / HEAD_DIM),
        name="attend",
    )(place, q, k, v, past, lw, table, *buckets)


def norm_kernel(slots, offsets, local_width, place_ref, gate_ref, gain_ref, *rest):
    pieces, (out_ref, gated) = rest[:-2], rest[-2:]
    square = None
    index = 0
    for s in range(slots):
        base = lax.rem(place_ref[0] + slots - s, slots) * local_width
        for offset in offsets:
            piece = pieces[index]
            index += 1
            cols = pl.ds(pl.multiple_of(base + offset, HEAD_DIM), piece.shape[1])
            gate = gate_ref[:, cols].astype(jnp.float32)
            value = piece[...].astype(jnp.float32) * (gate / (1.0 + jnp.exp(-gate)))
            gated[:, cols] = value
            here = jnp.sum(value * value, axis=1, keepdims=True)
            square = here if square is None else square + here
    factor = lax.rsqrt(square / gated.shape[1] + EPSILON)
    out_ref[...] = (gain_ref[...] * gated[...] * factor).astype(jnp.bfloat16)


def norm(place, gate, gain, pieces, slots, offsets, local_width):
    rows, width = gate.shape
    tile = min(rows, 64)
    return pl.pallas_call(
        functools.partial(norm_kernel, slots, offsets, local_width),
        grid_spec=pltpu.PrefetchScalarGridSpec(
            num_scalar_prefetch=1,
            grid=(rows // tile,),
            in_specs=[
                pl.BlockSpec((tile, width), lambda g, *_: (g, 0)),
                pl.BlockSpec((1, width), lambda g, *_: (0, 0)),
            ]
            + [pl.BlockSpec((tile, p.shape[1]), lambda g, *_: (g, 0)) for p in pieces],
            out_specs=pl.BlockSpec((tile, width), lambda g, *_: (g, 0)),
            scratch_shapes=[pltpu.VMEM((tile, width), jnp.float32)],
        ),
        out_shape=jax.ShapeDtypeStruct((rows, width), jnp.bfloat16),
        compiler_params=pltpu.CompilerParams(vmem_limit_bytes=VMEM),
        cost_estimate=cost(3.2),
        name="norm",
    )(place, gate, gain.reshape(1, width), *pieces)


def shifted(value, axis, steps):
    count = lax.axis_size(axis)
    return lax.ppermute(value, axis, [(i, (i + steps) % count) for i in range(count)])


def from_partner(value, axis, level, up=False):
    count = lax.axis_size(axis)
    return lax.ppermute(value, axis, [(i, i ^ 1 << level) for i in range(count) if not up or not i >> level & 1])


def added(left, right):
    return (left.astype(jnp.float32) + right.astype(jnp.float32)).astype(jnp.bfloat16)


def after(value, *earlier):
    return lax.optimization_barrier((value,) + earlier)[0]


def local(queries, key_vectors, values, level_weights, gate_branch, norm_gain):
    rows, local_width = queries.shape
    heads = local_width // HEAD_DIM
    near_n = rows.bit_length()
    levels = level_weights.shape[0]
    far_n = levels - near_n
    slots = lax.axis_size("heads")
    seq_place = lax.axis_index("seq")
    heads_place = lax.axis_index("heads")
    place = jnp.stack([heads_place, seq_place & 1, seq_place])
    unit = heads // 8
    sizes = [n * unit for n in SIZES] if heads % 8 == 0 else [1] * heads
    starts = [sum(sizes[:i]) for i in range(len(sizes))]
    step = min(sizes)

    coef = level_scale(jnp.arange(levels, dtype=jnp.int32)) * HEAD_DIM**-0.5
    far_id = jnp.arange(levels, dtype=jnp.int32) - near_n
    present = jnp.where(far_id < 0, 1, seq_place >> jnp.maximum(far_id, 0) & 1)
    coef = coef * present.astype(jnp.float32)
    lw = (level_weights * coef[:, None, None]).reshape(levels, heads // step, step, rows)
    lw = jnp.pad(jnp.transpose(lw, (1, 3, 2, 0)), ((0, 0), (0, 0), (0, 0), (0, LEVEL_LANES - levels)))
    lw = lw.reshape(heads // step, rows, step * LEVEL_LANES)
    lw = jnp.pad(lw, ((0, 0), (0, 0), (0, HEAD_DIM - step * LEVEL_LANES)))
    pos = jnp.arange(HEAD_DIM, dtype=jnp.int32)
    differ = pos[:, None] ^ pos[None, :]
    table = sum((differ >> b > 0).astype(jnp.int32) for b in range(HEAD_DIM.bit_length()))
    table = table + LEVEL_LANES * jnp.arange(step, dtype=jnp.int32)[:, None, None]
    table = jnp.where(pos[:, None] >= pos[None, :], table, HEAD_DIM - 1)

    past = []

    def send_until(count, *earlier):
        for index in range(len(past), min(count, len(sizes))):
            past.append(shifted(after(cuts[index], *earlier), "seq", 1))

    half = HEAD_DIM // 2
    states, cut = block_states(key_vectors, values, sizes[0])
    cuts = [cut]
    send_until(1)
    other = from_partner(states, "seq", 0)
    buckets = [other]
    running = lax.dynamic_slice_in_dim(added(states, other), (seq_place & 1) * half, half, 1)
    whole = lax.optimization_barrier((key_vectors, values, running))[:2]
    for start, size in zip(starts[1:], sizes[1:]):
        cols = slice(start * HEAD_DIM, (start + size) * HEAD_DIM)
        cuts.append(jnp.stack([w[:, cols] for w in whole]))
    for level in range(1, far_n):
        if level == 2:
            running = after(running, past[0])
        other = from_partner(running, "seq", level, level == far_n - 1)
        if level < far_n - 1:
            send_until(1 + level, running)
            running = added(running, other)
        buckets += [other, from_partner(other, "seq", 0)]
    send_until(len(sizes), other)

    kept = [[] for _ in range(slots)]
    latest = ()
    for index in range(len(sizes)):
        pieces = attend(
            place, queries, key_vectors, values, after(past[index], *latest), lw, table, buckets,
            starts[index], step, near_n, slots,
        )
        latest = (pieces[-1],)
        for s in range(slots):
            kept[s].append(pieces[s] if s == 0 else shifted(pieces[s], "heads", s))
    pieces = [piece for group in kept for piece in group]
    offsets = tuple(start * HEAD_DIM for start in starts)
    return norm(heads_place.reshape(1), gate_branch, norm_gain, pieces, slots, offsets, local_width)


def solution(mesh):
    return jax.shard_map(
        local,
        mesh=mesh,
        in_specs=(
            P("seq", "heads"),
            P("seq", "heads"),
            P("seq", "heads"),
            P(None, "heads", "seq"),
            P(("seq", "heads"), None),
            P(),
        ),
        out_specs=P(("seq", "heads"), None),
        check_vma=False,
    )
```

```python
import functools

import jax
import jax.numpy as jnp
from jax import lax
from jax.experimental import pallas as pl
from jax.experimental.pallas import tpu as pltpu
from jax.sharding import PartitionSpec as P

HEAD_DIM = 128
WINDOW = 512
EPSILON = 1e-06
LOG2E = 1.4426950408889634
LEVEL_LANES = 16
SIZES = (1, 2, 2, 1, 1, 1)
VMEM = 16 * 1024 * 1024
NN = (((1,), (0,)), ((), ()))
NT = (((1,), (1,)), ((), ()))
TN = (((0,), (0,)), ((), ()))


def mm(left, right, dims=NN):
    return lax.dot_general(left, right, dims, preferred_element_type=jnp.float32)


def level_scale(levels):
    return jnp.exp2(-0.5 * jnp.maximum(levels - 1, 0).astype(jnp.float32))


def joined(parts, axis):
    return parts[0] if len(parts) == 1 else jnp.concatenate(parts, axis)


def cost(micros):
    return pl.CostEstimate(
        flops=int(micros * 1.1e9), bytes_accessed=int(micros * 3.6e6), transcendentals=0
    )


def state_kernel(heads, k_ref, v_ref, out_ref, copy_ref):
    for h in range(heads):
        cols = slice(h * HEAD_DIM, (h + 1) * HEAD_DIM)
        out_ref[h] = mm(k_ref[:, cols], v_ref[:, cols], TN).astype(jnp.bfloat16)

    @pl.when(pl.program_id(0) == 0)
    def _():
        copy_ref[0] = k_ref[:, : copy_ref.shape[2]]
        copy_ref[1] = v_ref[:, : copy_ref.shape[2]]


def block_states(k, v, copied):
    rows, width = k.shape
    heads = width // HEAD_DIM
    step = heads // 2 if heads % 2 == 0 else heads
    block = pl.BlockSpec((rows, step * HEAD_DIM), lambda g: (0, g))
    copy_shape = (2, rows, copied * HEAD_DIM)
    return pl.pallas_call(
        functools.partial(state_kernel, step),
        grid=(heads // step,),
        in_specs=[block, block],
        out_specs=[pl.BlockSpec((step, HEAD_DIM, HEAD_DIM), lambda g: (g, 0, 0)), pl.BlockSpec(copy_shape, lambda g: (0, 0, 0))],
        out_shape=[
            jax.ShapeDtypeStruct((heads, HEAD_DIM, HEAD_DIM), jnp.bfloat16),
            jax.ShapeDtypeStruct(copy_shape, k.dtype),
        ],
        cost_estimate=cost(0.3 * heads),
        name="block_states",
    )(k, v)


def attend_kernel(qb, heads, near_n, slots, place_ref, q_ref, k_ref, v_ref, past_ref, lw_ref, table_ref, *rest):
    bucket_refs, out_refs, mixed = rest[: -1 - slots], rest[-1 - slots : -1], rest[-1]
    rows = q_ref.shape[0]
    odd = place_ref[1] == 1
    for h in range(heads):
        cols = slice(h * HEAD_DIM, (h + 1) * HEAD_DIM)
        buckets = [bucket_refs[0][h]]
        for mine_ref, theirs_ref in zip(bucket_refs[1::2], bucket_refs[2::2]):
            mine, theirs = mine_ref[h], theirs_ref[h]
            buckets += [jnp.where(odd, theirs, mine), jnp.where(odd, mine, theirs)]
        tensors = [ref.at[:, cols] for ref in (q_ref, k_ref, v_ref, past_ref.at[0], past_ref.at[1])]
        attend_head(qb, place_ref, *tensors, lw_ref, table_ref, joined(buckets, 0), mixed.at[:, cols], h, near_n)
    count = rows // slots
    for s in range(slots):
        start = pl.multiple_of(lax.rem(place_ref[0] + s, slots) * count, count)
        out_refs[s][...] = mixed[pl.ds(start, count), :].astype(jnp.bfloat16)


def attend_head(qb, place_ref, q_ref, k_ref, v_ref, kp_ref, vp_ref, lw_ref, table_ref, bucket, out_ref, head, near_n):
    lane = HEAD_DIM
    scale = HEAD_DIM**-0.5 * LOG2E
    bias = jnp.where(place_ref[2] == 0, -1e30, 0.0).astype(jnp.float32)
    table = table_ref[head]
    causal = lax.broadcasted_iota(jnp.int32, (qb, qb), 0) >= lax.broadcasted_iota(
        jnp.int32, (qb, qb), 1
    )
    lane_bits = lane.bit_length() - 1
    first_level = head * LEVEL_LANES
    far_n = bucket.shape[0] // lane
    bf = jnp.bfloat16
    q = q_ref[...]
    own_low = mm(q, k_ref[:qb, :], NT)
    own_high = mm(q[qb:], k_ref[qb:, :], NT)
    past_low = mm(q[:qb], kp_ref[:qb, :], NT) + bias
    past_high = mm(q, kp_ref[qb:, :], NT) + bias

    def softmax(edge_own, edge_past, full):
        edge = jnp.where(causal, edge_own, edge_past)
        top = jnp.max(jnp.maximum(edge, full), axis=1, keepdims=True)
        edge = jnp.exp2((edge - top) * scale)
        full = jnp.exp2((full - top) * scale)
        total = jnp.sum(edge + full, axis=1, keepdims=True)
        own = jnp.where(causal, edge, 0.0).astype(bf)
        return own, jnp.where(causal, 0.0, edge).astype(bf), full.astype(bf), 1.0 / total

    low_own, low_past, low_full, low_factor = softmax(own_low[:qb], past_low, past_high[:qb])
    high_own, high_past, high_full, high_factor = softmax(own_high, past_high[qb:], own_low[qb:])

    def near_weights(scores, row, column):
        out = []
        for a in range(row // lane, row // lane + qb // lane):
            mix = lw_ref[0, a * lane : (a + 1) * lane, :]
            parts = []
            for b in range(column // lane, column // lane + qb // lane):
                part = scores[a * lane - row : (a + 1) * lane - row, b * lane - column : (b + 1) * lane - column]
                if b < a:
                    level = first_level + lane_bits + (a ^ b).bit_length()
                    parts.append((part * mix[:, level : level + 1]).astype(bf))
                elif b == a:
                    parts.append((part * jnp.take_along_axis(mix, table, axis=1)).astype(bf))
                else:
                    parts.append(jnp.zeros((lane, lane), bf))
            out.append(joined(parts, 1))
        return joined(out, 0)

    first = mm(
        joined(
            [low_own, high_full, near_weights(own_low[:qb], 0, 0), near_weights(own_low[qb:], qb, 0)], 0
        ),
        v_ref[:qb, :],
    )
    second = mm(joined([high_own, near_weights(own_high, qb, qb)], 0), v_ref[qb:, :])
    third = mm(low_past, vp_ref[:qb, :])
    fourth = mm(joined([low_full, high_past], 0), vp_ref[qb:, :])
    proj = mm(q, joined([bucket[j*lane:(j+1)*lane] for j in range(far_n)], 1))
    far_rows = []
    for a in range(2 * qb // lane):
        inside = slice(a * lane, (a + 1) * lane)
        mix = lw_ref[0, inside, :]
        level = first_level + near_n
        total = None
        for j in range(far_n):
            t = proj[inside, j*lane:(j+1)*lane] * mix[:, level + j : level + j + 1]
            total = t if total is None else total + t
        far_rows.append(total)
    far = joined(far_rows, 0)
    out_ref[:qb, :] = (first[:qb] + third + fourth[:qb]) * low_factor + first[2 * qb : 3 * qb] + far[:qb]
    out_ref[qb:, :] = (
        (first[qb : 2 * qb] + second[:qb] + fourth[qb:]) * high_factor
        + first[3 * qb :]
        + second[qb:]
        + far[qb:]
    )


def attend(place, q, k, v, past, lw, table, buckets, head, step, near_n, slots):
    rows, width = past.shape[1:]
    cols = step * HEAD_DIM
    count = rows // slots
    whole = pl.BlockSpec((rows, cols), lambda g, *_: (0, head // step + g))
    group = lambda g, *_: (head // step + g, 0, 0)
    qb = rows // 2
    return pl.pallas_call(
        functools.partial(attend_kernel, qb, step, near_n, slots),
        grid_spec=pltpu.PrefetchScalarGridSpec(
            num_scalar_prefetch=1,
            grid=(width // cols,),
            in_specs=[
                whole,
                whole,
                whole,
                pl.BlockSpec((2, rows, cols), lambda g, *_: (0, 0, g)),
                pl.BlockSpec((1,) + lw.shape[1:], group),
                pl.BlockSpec(table.shape, lambda g, *_: (0, 0, 0)),
            ]
            + [pl.BlockSpec((step,) + b.shape[1:], group) for b in buckets],
            out_specs=[pl.BlockSpec((count, cols), lambda g, *_: (0, g))] * slots,
            scratch_shapes=[pltpu.VMEM((rows, cols), jnp.float32)],
        ),
        out_shape=[jax.ShapeDtypeStruct((count, width), jnp.bfloat16)] * slots,
        compiler_params=pltpu.CompilerParams(vmem_limit_bytes=VMEM),
        cost_estimate=cost(1.6 * width / HEAD_DIM),
        name="attend",
    )(place, q, k, v, past, lw, table, *buckets)


def norm_kernel(slots, offsets, local_width, place_ref, gate_ref, gain_ref, *rest):
    pieces, (out_ref, gated) = rest[:-2], rest[-2:]
    square = None
    index = 0
    for s in range(slots):
        base = lax.rem(place_ref[0] + slots - s, slots) * local_width
        for offset in offsets:
            piece = pieces[index]
            index += 1
            cols = pl.ds(pl.multiple_of(base + offset, HEAD_DIM), piece.shape[1])
            gate = gate_ref[:, cols].astype(jnp.float32)
            value = piece[...].astype(jnp.float32) * (gate / (1.0 + jnp.exp(-gate)))
            gated[:, cols] = value
            here = jnp.sum(value * value, axis=1, keepdims=True)
            square = here if square is None else square + here
    factor = lax.rsqrt(square / gated.shape[1] + EPSILON)
    out_ref[...] = (gain_ref[...] * gated[...] * factor).astype(jnp.bfloat16)


def norm(place, gate, gain, pieces, slots, offsets, local_width):
    rows, width = gate.shape
    tile = min(rows, 64)
    return pl.pallas_call(
        functools.partial(norm_kernel, slots, offsets, local_width),
        grid_spec=pltpu.PrefetchScalarGridSpec(
            num_scalar_prefetch=1,
            grid=(rows // tile,),
            in_specs=[
                pl.BlockSpec((tile, width), lambda g, *_: (g, 0)),
                pl.BlockSpec((1, width), lambda g, *_: (0, 0)),
            ]
            + [pl.BlockSpec((tile, p.shape[1]), lambda g, *_: (g, 0)) for p in pieces],
            out_specs=pl.BlockSpec((tile, width), lambda g, *_: (g, 0)),
            scratch_shapes=[pltpu.VMEM((tile, width), jnp.float32)],
        ),
        out_shape=jax.ShapeDtypeStruct((rows, width), jnp.bfloat16),
        compiler_params=pltpu.CompilerParams(vmem_limit_bytes=VMEM),
        cost_estimate=cost(3.2),
        name="norm",
    )(place, gate, gain.reshape(1, width), *pieces)


def shifted(value, axis, steps):
    count = lax.axis_size(axis)
    return lax.ppermute(value, axis, [(i, (i + steps) % count) for i in range(count)])


def from_partner(value, axis, level, up=False):
    count = lax.axis_size(axis)
    return lax.ppermute(value, axis, [(i, i ^ 1 << level) for i in range(count) if not up or not i >> level & 1])


def added(left, right):
    return (left.astype(jnp.float32) + right.astype(jnp.float32)).astype(jnp.bfloat16)


def after(value, *earlier):
    return lax.optimization_barrier((value,) + earlier)[0]


def local(queries, key_vectors, values, level_weights, gate_branch, norm_gain):
    rows, local_width = queries.shape
    heads = local_width // HEAD_DIM
    near_n = rows.bit_length()
    levels = level_weights.shape[0]
    far_n = levels - near_n
    slots = lax.axis_size("heads")
    seq_place = lax.axis_index("seq")
    heads_place = lax.axis_index("heads")
    place = jnp.stack([heads_place, seq_place & 1, seq_place])
    unit = heads // 8
    sizes = [n * unit for n in SIZES] if heads % 8 == 0 else [1] * heads
    starts = [sum(sizes[:i]) for i in range(len(sizes))]
    step = min(sizes)

    coef = level_scale(jnp.arange(levels, dtype=jnp.int32)) * HEAD_DIM**-0.5
    far_id = jnp.arange(levels, dtype=jnp.int32) - near_n
    present = jnp.where(far_id < 0, 1, seq_place >> jnp.maximum(far_id, 0) & 1)
    coef = coef * present.astype(jnp.float32)
    lw = (level_weights * coef[:, None, None]).reshape(levels, heads // step, step, rows)
    lw = jnp.pad(jnp.transpose(lw, (1, 3, 2, 0)), ((0, 0), (0, 0), (0, 0), (0, LEVEL_LANES - levels)))
    lw = lw.reshape(heads // step, rows, step * LEVEL_LANES)
    lw = jnp.pad(lw, ((0, 0), (0, 0), (0, HEAD_DIM - step * LEVEL_LANES)))
    pos = jnp.arange(HEAD_DIM, dtype=jnp.int32)
    differ = pos[:, None] ^ pos[None, :]
    table = sum((differ >> b > 0).astype(jnp.int32) for b in range(HEAD_DIM.bit_length()))
    table = table + LEVEL_LANES * jnp.arange(step, dtype=jnp.int32)[:, None, None]
    table = jnp.where(pos[:, None] >= pos[None, :], table, HEAD_DIM - 1)

    past = []

    def send_until(count, *earlier):
        for index in range(len(past), min(count, len(sizes))):
            count = lax.axis_size("seq")
            pairs = [(i, (i + 1) % count) for i in range(count if index not in (len(sizes) - 2, len(sizes) - 1) else count - 1)]
            past.append(lax.ppermute(after(cuts[index], *earlier), "seq", pairs))

    half = HEAD_DIM // 2
    states, cut = block_states(key_vectors, values, sizes[0])
    cuts = [cut]
    send_until(1)
    other = from_partner(states, "seq", 0)
    buckets = [other]
    running = lax.dynamic_slice_in_dim(added(states, other), (seq_place & 1) * half, half, 1)
    whole = lax.optimization_barrier((key_vectors, values, running))[:2]
    for start, size in zip(starts[1:], sizes[1:]):
        cols = slice(start * HEAD_DIM, (start + size) * HEAD_DIM)
        cuts.append(jnp.stack([w[:, cols] for w in whole]))
    for level in range(1, far_n):
        if level == 2:
            running = after(running, past[0])
        other = from_partner(running, "seq", level, level == far_n - 1)
        if level < far_n - 1:
            send_until(2, running)
            running = added(running, other)
        buckets += [other, from_partner(other, "seq", 0)]
    send_until(len(sizes), other)

    kept = [[] for _ in range(slots)]
    latest = ()
    for index in range(len(sizes)):
        pieces = attend(
            place, queries, key_vectors, values, after(past[index], *latest), lw, table, buckets,
            starts[index], step, near_n, slots,
        )
        latest = (pieces[-1],)
        for s in range(slots):
            kept[s].append(pieces[s] if s == 0 else shifted(pieces[s], "heads", s))
    pieces = [piece for group in kept for piece in group]
    offsets = tuple(start * HEAD_DIM for start in starts)
    return norm(heads_place.reshape(1), gate_branch, norm_gain, pieces, slots, offsets, local_width)


def solution(mesh):
    return jax.shard_map(
        local,
        mesh=mesh,
        in_specs=(
            P("seq", "heads"),
            P("seq", "heads"),
            P("seq", "heads"),
            P(None, "heads", "seq"),
            P(("seq", "heads"), None),
            P(),
        ),
        out_specs=P(("seq", "heads"), None),
        check_vma=False,
    )
```
